32 devices in a mesh: shard: 4 (over y, core), ctx: 4 (over z), tp: 2 (over x).
Axes of the slice: x: 2, y: 2, z: 4, core: 2. Of those that a mesh axis runs over, the one named last changes fastest.
Arguments:
- hidden: bfloat16 [16, 1024, 1024], P('shard', 'ctx'), may hold values from -6 to 6
- cotangent: bfloat16 [16, 1024, 1024], P('shard', 'ctx'), may hold values from -6 to 6
- segment_ids: int32 [16, 1024], P('shard', 'ctx'), may hold values from 0 to 6, as said below
- adapter_ids: int32 [16], P('shard'), may hold values from 0 to 7, as said below
- norm_gain: float32 [1024], replicated, may hold values from 0.5 to 1.5
- proj_zx: bfloat16 [1024, 2, 2048], P('shard', None, 'tp'), may hold values from -0.1875 to 0.1875
- proj_bc: bfloat16 [1024, 256], P('shard'), may hold values from -0.1875 to 0.1875
- proj_dt: bfloat16 [1024, 32], P('shard', 'tp'), may hold values from -0.1875 to 0.1875
- proj_out: bfloat16 [1024, 2048], P('shard', 'tp'), may hold values from -0.125 to 0.125
- conv_x: float32 [4, 2048], P(None, 'tp'), may hold values from -3 to 3
- conv_x_bias: float32 [2048], P('tp'), may hold values from -3 to 3
- conv_bc: float32 [4, 256], replicated, may hold values from -3 to 3
- conv_bc_bias: float32 [256], replicated, may hold values from -3 to 3
- dt_bias: float32 [32], P('tp'), may hold values from -7 to -2
- decay_log: float32 [32], P('tp'), may hold values from -3 to 1.5
- skip_gain: float32 [32], P('tp'), may hold values from 0.5 to 1.5
- gate_gain: float32 [2048], P('tp'), may hold values from 0.5 to 1.5
- in_down: float32 [8, 1024, 16], P('shard'), may hold values from -0.1875 to 0.1875
- in_up: float32 [8, 16, 2, 2048], P('shard', None, None, 'tp'), may hold values from -0.5 to 0.5
- out_down: float32 [8, 2048, 16], P('shard', 'tp'), may hold values from -0.125 to 0.125
- out_up: float32 [8, 16, 1024], P('shard'), may hold values from -0.5 to 0.5
- in_down_m: float32 [8, 1024, 16], P('shard'), may hold values from -45.254833 to 45.254833
- in_up_m: float32 [8, 16, 2, 2048], P('shard', None, None, 'tp'), may hold values from -11.313708 to 11.313708
- out_down_m: float32 [8, 2048, 16], P('shard', 'tp'), may hold values from -67.88225 to 67.88225
- out_up_m: float32 [8, 16, 1024], P('shard'), may hold values from -22.627417 to 22.627417
- in_down_v: float32 [8, 1024, 16], P('shard'), may hold values from 81.92 to 327.68
- in_up_v: float32 [8, 16, 2, 2048], P('shard', None, None, 'tp'), may hold values from 5.12 to 20.48
- out_down_v: float32 [8, 2048, 16], P('shard', 'tp'), may hold values from 184.32 to 737.28
- out_up_v: float32 [8, 16, 1024], P('shard'), may hold values from 20.48 to 81.92
Outputs:
- output: bfloat16 [16, 1024, 1024], P('shard', 'ctx')
- input_grad: bfloat16 [16, 1024, 1024], P('shard', 'ctx')
- in_down_new: float32 [8, 1024, 16], P('shard')
- in_up_new: float32 [8, 16, 2, 2048], P('shard', None, None, 'tp')
- out_down_new: float32 [8, 2048, 16], P('shard', 'tp')
- out_up_new: float32 [8, 16, 1024], P('shard')
- in_down_m_new: float32 [8, 1024, 16], P('shard')
- in_up_m_new: float32 [8, 16, 2, 2048], P('shard', None, None, 'tp')
- out_down_m_new: float32 [8, 2048, 16], P('shard', 'tp')
- out_up_m_new: float32 [8, 16, 1024], P('shard')
- in_down_v_new: float32 [8, 1024, 16], P('shard')
- in_up_v_new: float32 [8, 16, 2, 2048], P('shard', None, None, 'tp')
- out_down_v_new: float32 [8, 2048, 16], P('shard', 'tp')
- out_up_v_new: float32 [8, 16, 1024], P('shard')
The draws below stay inside these ranges and needn't reach their ends.
Inputs may be any that keep to these rules, and one draw needn't show every extreme that they name: `segment_ids`: within a sequence the numbers never fall, start at 0 and end at 6; on each index of shard one of its 4 sequences has a document with positions on the first and on the last index of ctx. `adapter_ids`: on each index of shard the 4 sequences take consecutive adapter numbers, counted round modulo 8, from a first one drawn for that index.
All inputs are finite; a program needn't handle non-finite values.
Results may differ from the reference program's by a relative error of at most 0.0095.
Values may be sent and summed in bfloat16 or wider, within the bound.
No kernel may reach another device: no remote copies, remote signals or barrier semaphores. Data moves between devices by JAX's collectives and lax.ppermute only.
A program may use at most 256 MiB of HBM per device.

```python
import math
import jax
import jax.numpy as jnp
from jax import lax

D = 1024
HEADS = 32
HEADDIM = 64
STATE = 128
CONV = 4
STRETCH = 256
RANK = 16
ADAPT = 8
STEP = 10
TOK_DEV = 256
SEQ_DEV = 4
INNER = 2048
SEQS = 16
LEN = 1024
TOK_ADAPT = 2048


def draw_segment_ids(key, part):
    key = jax.random.fold_in(key, 11)
    free_key, side_key, pick_key = jax.random.split(key, 3)
    anywhere = jax.random.randint(free_key, (SEQS, 6), 1, LEN)
    edge_draw = jax.random.randint(side_key, (SEQS, 6), 0, 2 * (TOK_DEV - 1))
    near_edges = jnp.where(edge_draw < TOK_DEV - 1, 1 + edge_draw, LEN - TOK_DEV + 1 + edge_draw - (TOK_DEV - 1))
    chosen = jax.random.randint(pick_key, (SEQS // SEQ_DEV, 1), 0, SEQ_DEV)
    slot_index = (jnp.arange(SEQS) % SEQ_DEV).reshape(SEQS // SEQ_DEV, SEQ_DEV)
    spanning = (slot_index == chosen).reshape(SEQS, 1)
    bounds = jnp.where(spanning, near_edges, anywhere)
    positions = jnp.arange(LEN)
    return jnp.sum((bounds[:, None, :] <= positions[None, :, None]).astype(jnp.int32), axis=2).astype(jnp.int32)


def draw_adapter_ids(key, part):
    key = jax.random.fold_in(key, 23)
    groups = SEQS // SEQ_DEV
    first_ids = jax.random.randint(key, (groups,), 0, ADAPT)
    slot_index = jnp.arange(SEQS) % SEQ_DEV
    group_index = jnp.arange(SEQS) // SEQ_DEV
    return ((first_ids[group_index] + slot_index) % ADAPT).astype(jnp.int32)


def shard_levels(key, dims, shards, least, top_value):
    factor_of, own = 1.0, jax.random.fold_in(key, 6)
    for position, blocks in shards:
        steps = jnp.exp(jax.random.uniform(jax.random.fold_in(own, position), (blocks,), jnp.float32, least / len(shards), top_value / len(shards)))
        factor_of = factor_of * jnp.repeat(steps, dims[position] // blocks).reshape([-1 if axis == position else 1 for axis in range(len(dims))])
    return factor_of


def centred(rng, extent, scale, limit, cuts=(), kind=jnp.bfloat16):
    drawn = scale * jax.random.normal(rng, extent, jnp.float32)
    if cuts:
        drawn = drawn * shard_levels(rng, extent, cuts, -0.22, 0.18)
    return jnp.clip(drawn, -limit, limit).astype(kind)


def setup_inputs(seed: int = 0) -> dict:
    key_list = jax.random.split(jax.random.key(seed), 30)
    hidden = centred(key_list[0], (SEQS, LEN, D), 1.0, 6.0, ((0, 4), (1, 4)))
    cotangent = centred(key_list[1], (SEQS, LEN, D), 1.0, 6.0, ((0, 4), (1, 4)))
    segment_ids = draw_segment_ids(jax.random.fold_in(key_list[29], 71), 0)
    adapter_ids = draw_adapter_ids(jax.random.fold_in(key_list[29], 71), 0)
    norm_gain = jnp.clip(1.0 + 0.1 * jax.random.normal(key_list[4], (D,), jnp.float32), 0.5, 1.5)
    proj_zx = centred(key_list[5], (D, 2, INNER), D ** -0.5, 0.1875, ((0, 4), (2, 2)))
    proj_bc = centred(key_list[6], (D, 2 * STATE), D ** -0.5, 0.1875, ((0, 4),))
    proj_dt = centred(key_list[7], (D, HEADS), D ** -0.5, 0.1875, ((0, 4), (1, 2)))
    proj_out = centred(key_list[8], (D, INNER), INNER ** -0.5, 0.125, ((0, 4), (1, 2)))
    conv_x = centred(key_list[9], (CONV, INNER), CONV ** -0.5, 3.0, ((1, 2),), jnp.float32)
    conv_x_bias = centred(key_list[10], (INNER,), 0.5, 3.0, ((0, 2),), jnp.float32)
    conv_bc = centred(key_list[11], (CONV, 2 * STATE), CONV ** -0.5, 3.0, (), jnp.float32)
    conv_bc_bias = centred(key_list[12], (2 * STATE,), 0.5, 3.0, (), jnp.float32)
    dt_bias = jnp.clip(-7.0 + 5.0 * jax.random.uniform(key_list[13], (HEADS,), jnp.float32) ** shard_levels(key_list[13], (HEADS,), ((0, 2),), -0.2, 0.2), -7.0, -2.0)
    decay_log = jnp.clip(-3.0 + 4.5 * jax.random.uniform(key_list[14], (HEADS,), jnp.float32) ** shard_levels(key_list[14], (HEADS,), ((0, 2),), -0.2, 0.2), -3.0, 1.5)
    skip_gain = jnp.clip(0.5 + 1.0 * jax.random.uniform(key_list[15], (HEADS,), jnp.float32) ** shard_levels(key_list[15], (HEADS,), ((0, 2),), -0.2, 0.2), 0.5, 1.5)
    gate_gain = jnp.clip(1.0 + 0.1 * jax.random.normal(key_list[16], (INNER,), jnp.float32), 0.5, 1.5)
    in_down = centred(key_list[17], (ADAPT, D, RANK), D ** -0.5, 0.1875, ((0, 4),), jnp.float32)
    in_up = centred(key_list[18], (ADAPT, RANK, 2, INNER), (9 * RANK) ** -0.5, 0.5, ((0, 4), (3, 2)), jnp.float32)
    out_down = centred(key_list[19], (ADAPT, INNER, RANK), INNER ** -0.5, 0.125, ((0, 4), (1, 2)), jnp.float32)
    out_up = centred(key_list[20], (ADAPT, RANK, D), (9 * RANK) ** -0.5, 0.5, ((0, 4),), jnp.float32)
    in_down_m = centred(key_list[21], (ADAPT, D, RANK), (0.22 * TOK_ADAPT ** 0.5), 45.254833, ((0, 4),), jnp.float32)
    in_up_m = centred(key_list[22], (ADAPT, RANK, 2, INNER), (0.055 * TOK_ADAPT ** 0.5), 11.313708, ((0, 4), (3, 2)), jnp.float32)
    out_down_m = centred(key_list[23], (ADAPT, INNER, RANK), (0.33 * TOK_ADAPT ** 0.5), 67.88225, ((0, 4), (1, 2)), jnp.float32)
    out_up_m = centred(key_list[24], (ADAPT, RANK, D), (0.11 * TOK_ADAPT ** 0.5), 22.627417, ((0, 4),), jnp.float32)
    in_down_v = jnp.clip(jnp.exp(math.log(327.68) - 1.3862944 * jax.random.uniform(key_list[25], (ADAPT, D, RANK), jnp.float32) ** shard_levels(key_list[25], (ADAPT, D, RANK), ((0, 4),), -0.2, 0.2)), 81.92, 327.68)
    in_up_v = jnp.clip(jnp.exp(math.log(20.48) - 1.3862944 * jax.random.uniform(key_list[26], (ADAPT, RANK, 2, INNER), jnp.float32) ** shard_levels(key_list[26], (ADAPT, RANK, 2, INNER), ((0, 4), (3, 2)), -0.2, 0.2)), 5.12, 20.48)
    out_down_v = jnp.clip(jnp.exp(math.log(737.28) - 1.3862944 * jax.random.uniform(key_list[27], (ADAPT, INNER, RANK), jnp.float32) ** shard_levels(key_list[27], (ADAPT, INNER, RANK), ((0, 4), (1, 2)), -0.2, 0.2)), 184.32, 737.28)
    out_up_v = jnp.clip(jnp.exp(math.log(81.92) - 1.3862944 * jax.random.uniform(key_list[28], (ADAPT, RANK, D), jnp.float32) ** shard_levels(key_list[28], (ADAPT, RANK, D), ((0, 4),), -0.2, 0.2)), 20.48, 81.92)
    return {"hidden": hidden, "cotangent": cotangent, "segment_ids": segment_ids, "adapter_ids": adapter_ids, "norm_gain": norm_gain, "proj_zx": proj_zx, "proj_bc": proj_bc, "proj_dt": proj_dt, "proj_out": proj_out, "conv_x": conv_x, "conv_x_bias": conv_x_bias, "conv_bc": conv_bc, "conv_bc_bias": conv_bc_bias, "dt_bias": dt_bias, "decay_log": decay_log, "skip_gain": skip_gain, "gate_gain": gate_gain, "in_down": in_down, "in_up": in_up, "out_down": out_down, "out_up": out_up, "in_down_m": in_down_m, "in_up_m": in_up_m, "out_down_m": out_down_m, "out_up_m": out_up_m, "in_down_v": in_down_v, "in_up_v": in_up_v, "out_down_v": out_down_v, "out_up_v": out_up_v}


norm_eps = 1e-05
beta_one = 0.9
beta_two = 0.99
adam_eps = 1e-08
weight_decay = 0.01
rate_down = 0.02
rate_up = 0.05
highest = lax.Precision.HIGHEST

@jax.custom_vjp
def low(v):
    return lax.optimization_barrier(v.astype(jnp.bfloat16)).astype(jnp.float32)

@jax.custom_vjp
def low_back(v):
    return v

def low_keep(v):
    return (low(v), None)

def low_pass(kept, grad):
    return (grad,)

def back_keep(v):
    return (v, None)

def back_low(kept, grad):
    return (low(grad),)
low.defvjp(low_keep, low_pass)
low_back.defvjp(back_keep, back_low)

def matmul(left, right):
    return jnp.dot(left, right, precision=highest, preferred_element_type=jnp.float32)

def rms_scale(values):
    return lax.rsqrt(lax.optimization_barrier(jnp.mean(values * values, axis=-1, keepdims=True)) + norm_eps)

def conv_rows(extended, seg_ext, kernel, conv_bias, tok_count):
    kernel_len = kernel.shape[0]
    segment = seg_ext[:, kernel_len - 1:]
    summed = conv_bias + kernel[kernel_len - 1] * extended[:, kernel_len - 1:]
    for offset in range(1, kernel_len):
        first_row = kernel_len - 1 - offset
        earlier = extended[:, first_row:first_row + tok_count]
        matching = (seg_ext[:, first_row:first_row + tok_count] == segment).astype(jnp.float32)
        summed = summed + kernel[first_row] * earlier * matching[:, :, None]
    return summed

def stretch_mix(carried, block):
    x_values, b_values, c_values, step_sizes, log_decay, segment, seg_before = block
    span_len = segment.shape[1]
    cumul = jnp.cumsum(log_decay, axis=1)
    row_index = lax.broadcasted_iota(jnp.int32, (span_len, span_len), 0)
    col_index = lax.broadcasted_iota(jnp.int32, (span_len, span_len), 1)
    causal = (col_index <= row_index)[None, :, :, None]
    allowed = causal & (segment[:, :, None] == segment[:, None, :])[..., None]
    log_gaps = cumul[:, :, None, :] - cumul[:, None, :, :]
    decays = jnp.where(allowed, jnp.exp(jnp.where(causal, log_gaps, 0.0)), 0.0)
    scores = jnp.einsum('stn,sun->stu', c_values, b_values, precision=highest)
    scaled = x_values * step_sizes[..., None]
    weighted = decays * scores[..., None]
    inside = jnp.einsum('stuh,suhp->sthp', weighted, scaled, precision=highest)
    keep_in = (segment == seg_before[:, None]).astype(jnp.float32)[..., None] * jnp.exp(cumul)
    carried_in = jnp.einsum('stn,shpn->sthp', c_values, carried, precision=highest) * keep_in[..., None]
    last_seg = segment[:, -1:]
    tail_decay = jnp.exp(cumul[:, -1:, :] - cumul) * (segment == last_seg).astype(jnp.float32)[..., None]
    contrib = jnp.einsum('sth,sthp,stn->shpn', tail_decay, scaled, b_values, precision=highest)
    stretch_decay = jnp.exp(cumul[:, -1, :]) * (last_seg == seg_before[:, None]).astype(jnp.float32)
    new_state = stretch_decay[..., None, None] * carried + contrib
    return (new_state, inside + carried_in)

def stretch_scan(carried, x_values, b_values, c_values, step_sizes, log_decay, segment, token_before):
    seq_count, length = segment.shape
    pieces = length // STRETCH

    def to_blocks(values):
        return jnp.moveaxis(values.reshape((seq_count, pieces, STRETCH) + values.shape[2:]), 1, 0)
    starts = jnp.moveaxis(token_before.reshape(seq_count, pieces, STRETCH)[:, :, 0], 1, 0)
    blocks = (to_blocks(x_values), to_blocks(b_values), to_blocks(c_values), to_blocks(step_sizes), to_blocks(log_decay), to_blocks(segment), starts)
    last_state, results = lax.scan(jax.checkpoint(stretch_mix), carried, blocks)
    return (last_state, jnp.moveaxis(results, 0, 1).reshape(x_values.shape))

def block_forward(frozen, segment, row_data, down_a, up_a, down_b, up_b):
    norm_gain, proj_zx, proj_bc, proj_dt, proj_out, kernel, conv_all_bias, dt_bias, decay_log, skip_gain, gate_gain = frozen
    normed = low(row_data * rms_scale(row_data) * norm_gain)
    ranked = low(low_back(matmul(normed, low(down_a))))
    both = matmul(normed, proj_zx.reshape(D, 2 * INNER)) + matmul(ranked, low(up_a).reshape(RANK, 2 * INNER))
    both = low(low_back(both))
    gates = both[:, :INNER]
    maps = low(low_back(matmul(normed, proj_bc)))
    raw_steps = low(low_back(matmul(normed, proj_dt)))
    mix_in = jnp.concatenate([both[:, INNER:], maps], axis=1)
    seg_ext = jnp.concatenate([jnp.full((CONV - 1,), -1, jnp.int32), segment]).astype(jnp.int32)
    padded = jnp.concatenate([jnp.zeros((CONV - 1, mix_in.shape[1]), jnp.float32), mix_in], axis=0)
    convolved = jax.nn.silu(conv_rows(padded[None], seg_ext[None], kernel, conv_all_bias, LEN))[0]
    x_values = convolved[:, :INNER].reshape(LEN, HEADS, HEADDIM)
    b_values = convolved[:, INNER:INNER + STATE]
    c_values = convolved[:, INNER + STATE:]
    step_sizes = jax.nn.softplus(raw_steps + dt_bias)
    log_decay = -jnp.exp(decay_log) * step_sizes
    token_before = seg_ext[CONV - 2:CONV - 2 + LEN]
    zero_state = jnp.zeros((1, HEADS, HEADDIM, STATE), jnp.float32)
    last_state, mixed = stretch_scan(zero_state, x_values[None], b_values[None], c_values[None], step_sizes[None], log_decay[None], segment[None], token_before[None])
    mixed = mixed[0] + skip_gain[:, None] * x_values
    gated = mixed.reshape(LEN, INNER) * jax.nn.silu(gates)
    out_normed = low(gated * rms_scale(gated) * gate_gain)
    small = low(low_back(matmul(out_normed, low(down_b))))
    projected = lax.dot_general(out_normed, proj_out, (((1,), (1,)), ((), ())), precision=highest, preferred_element_type=jnp.float32)
    return row_data + projected + matmul(small, low(up_b))

def adam_update(weight, first, second, gradient, rate):
    first_new = beta_one * first + (1.0 - beta_one) * gradient
    second_new = beta_two * second + (1.0 - beta_two) * gradient * gradient
    first_hat = first_new / (1.0 - beta_one ** STEP)
    second_hat = second_new / (1.0 - beta_two ** STEP)
    weight_new = weight - rate * (first_hat / (jnp.sqrt(second_hat) + adam_eps) + weight_decay * weight)
    return (weight_new, first_new, second_new)

def reference(hidden, cotangent, segment_ids, adapter_ids, norm_gain, proj_zx, proj_bc, proj_dt, proj_out, conv_x, conv_x_bias, conv_bc, conv_bc_bias, dt_bias, decay_log, skip_gain, gate_gain, in_down, in_up, out_down, out_up, in_down_m, in_up_m, out_down_m, out_up_m, in_down_v, in_up_v, out_down_v, out_up_v):
    kernel = jnp.concatenate([conv_x, conv_bc], axis=1)
    conv_all_bias = jnp.concatenate([conv_x_bias, conv_bc_bias])
    frozen = (norm_gain, proj_zx.astype(jnp.float32), proj_bc.astype(jnp.float32), proj_dt.astype(jnp.float32), proj_out.astype(jnp.float32), kernel, conv_all_bias, dt_bias, decay_log, skip_gain, gate_gain)
    masters = (in_down, in_up, out_down, out_up)

    def per_sequence(totals, packed):
        hidden_row, cot_row, segment, chosen = packed
        picked = tuple((lax.dynamic_index_in_dim(adapter_table, chosen, 0, keepdims=False) for adapter_table in masters))

        def forward(row_data, down_a, up_a, down_b, up_b):
            return block_forward(frozen, segment, row_data, down_a, up_a, down_b, up_b)
        result, pullback = jax.vjp(forward, hidden_row.astype(jnp.float32), *picked)
        gradients = pullback(cot_row.astype(jnp.float32))
        updated = tuple((lax.dynamic_update_index_in_dim(summed, lax.dynamic_index_in_dim(summed, chosen, 0, keepdims=False) + piece_grad, chosen, 0) for summed, piece_grad in zip(totals, gradients[1:])))
        return (updated, (result.astype(jnp.bfloat16), gradients[0].astype(jnp.bfloat16)))
    starting = tuple((jnp.zeros(adapter_table.shape, jnp.float32) for adapter_table in masters))
    totals, outputs = lax.scan(per_sequence, starting, (hidden, cotangent, segment_ids, adapter_ids))
    output, input_grad = outputs
    down_in = adam_update(in_down, in_down_m, in_down_v, totals[0], rate_down)
    up_in = adam_update(in_up, in_up_m, in_up_v, totals[1], rate_up)
    down_out = adam_update(out_down, out_down_m, out_down_v, totals[2], rate_down)
    up_out = adam_update(out_up, out_up_m, out_up_v, totals[3], rate_up)
    return (output, input_grad, down_in[0], up_in[0], down_out[0], up_out[0], down_in[1], up_in[1], down_out[1], up_out[1], down_in[2], up_in[2], down_out[2], up_out[2])
```

```python
import functools

import jax
import jax.numpy as jnp
import numpy as np
from jax import lax
from jax.experimental import pallas as pl
from jax.experimental.pallas import tpu as pltpu
from jax.sharding import PartitionSpec as P

STEP = 10
HALO = 16
LANES = 128
TILE = 256
LOG2E = 1.4426950408889634

norm_eps = 1e-05
beta_one = 0.9
beta_two = 0.99
adam_eps = 1e-08
weight_decay = 0.01
rate_down = 0.02
rate_up = 0.05
f32 = jnp.float32
bf16 = jnp.bfloat16
VMEM_BYTES = 8 * 1024 * 1024

NN = (((1,), (0,)), ((), ()))
NT = (((1,), (1,)), ((), ()))
TN = (((0,), (0,)), ((), ()))


def dot(left, right, dims=NN):
    return lax.dot_general(left, right, dims, preferred_element_type=f32)


def iota(shape, axis):
    return lax.broadcasted_iota(jnp.int32, shape, axis)


def sigmoid(v):
    return 0.5 + 0.5 * jnp.tanh(0.5 * v)


def split_heads(values, heads):
    high = values.astype(bf16).astype(f32)
    rest = values - high
    middle = rest.astype(bf16).astype(f32)
    least = rest - middle
    return (high + pltpu.roll(middle, heads, 1) + pltpu.roll(least, 2 * heads, 1)).astype(bf16)


def running_sum(values, backward=False):
    count = values.shape[0]
    row = iota(values.shape, 0)
    step = 1
    while step < count:
        if backward:
            moved = jnp.where(row < count - step, pltpu.roll(values, count - step, 0), 0.0)
        else:
            moved = jnp.where(row >= step, pltpu.roll(values, step, 0), 0.0)
        values = values + moved
        step *= 2
    return values


def tile_at(index):
    if isinstance(index, int):
        return slice(index * TILE, (index + 1) * TILE)
    return pl.ds(pl.multiple_of(index * TILE, TILE), TILE)


def causal_same(seg_col, seg_row, transposed):
    count = seg_row.shape[1]
    rows, cols = iota((count, count), 0), iota((count, count), 1)
    order = (rows <= cols) if transposed else (cols <= rows)
    return order & (seg_col == seg_row)


class Sizes:
    def __init__(self, hidden, proj_zx, conv_bc, dt_bias, in_down, shards, parts):
        self.seqs_loc, self.toks, self.width = hidden.shape
        self.parts, self.shards = parts, shards
        self.seqs = self.seqs_loc // parts
        self.depth = proj_zx.shape[0]
        self.inner_loc = proj_zx.shape[2]
        self.inner = self.inner_loc * parts
        self.heads_loc = dt_bias.shape[0]
        self.head_size = self.inner_loc // self.heads_loc
        self.state = conv_bc.shape[1] // 2
        self.rank = in_down.shape[2]
        self.owned = in_down.shape[0]
        self.ext = self.toks + HALO
        self.tiles = self.inner_loc // TILE
        self.heads_tile = TILE // self.head_size
        self.table_rows = self.owned * self.rank


class Gather:
    def __init__(self, value):
        self.count = lax.axis_size("shard")
        self.far = range(2, self.count, 2)
        self.own, self.other = {0: value}, {}

    def far_own(self, *earlier):
        for r in self.far:
            high = 1 << (r.bit_length() - 1)
            self.own[r] = swap_shards(after(self.own[r ^ high], *earlier), high)

    def part(self, value, *earlier):
        self.other[0] = swap_parts(after(value, *earlier))

    def far_by_part(self, rows, *earlier):
        for r in self.far:
            self.other[r] = swap_parts(after(self.own[r][:rows], *earlier))

    def far_by_shard(self, *earlier):
        for r in self.far:
            high = 1 << (r.bit_length() - 1)
            self.other[r] = swap_shards(after(self.other[r ^ high], *earlier), high)

    def far_top(self, cut, *earlier):
        self.top = {r: swap_parts(after(self.own[r][:cut], *earlier)) for r in self.far}

    def far_bottom(self, cut, *earlier):
        self.bottom = {0: self.other[0][cut:]}
        for r in self.far:
            high = 1 << (r.bit_length() - 1)
            self.bottom[r] = swap_shards(after(self.bottom[r ^ high], *earlier), high)
        del self.bottom[0]

    def near(self, blocks, far, *earlier):
        for r in self.far if far else [0]:
            blocks[r + 1] = swap_shards(after(blocks[r], *earlier), 1)

    def blocks(self, blocks):
        return [blocks[r] for r in range(self.count)]

    def halves(self, part, cut):
        if part == 0:
            every = self.blocks(self.own)
            return every, every, [cut] * self.count
        tops = [self.top.get(r, self.other.get(r)) for r in range(self.count)]
        bottoms = [self.bottom.get(r, self.other.get(r)) for r in range(self.count)]
        return tops, bottoms, [0 if r in self.bottom else cut for r in range(self.count)]


def views(refs, offsets):
    return [ref.at[pl.ds(off, ref.shape[0] - off), :] if off else ref for ref, off in zip(refs, offsets)]


def table(z, blocks, base, adapter, me, width):
    chosen = lax.bitwise_xor(adapter // z.owned, me)
    row = pl.multiple_of(base + z.rank * lax.rem(adapter, z.owned), z.rank)
    total = None
    for r in range(z.shards):
        piece = jnp.where(chosen == r, blocks[r][pl.ds(row, z.rank), 0:width].astype(f32), 0.0)
        total = piece if total is None else total + piece
    return total.astype(bf16)


def shard_cols(z, me, r):
    return pl.ds(pl.multiple_of(lax.bitwise_xor(me, r) * z.depth, z.depth), z.depth)


def project(z, blocks, me, values, cols):
    total = None
    for r in range(z.shards):
        term = dot(values[:, shard_cols(z, me, r)], blocks[r][0 : z.depth, cols])
        total = term if total is None else total + term
    return total


def own_seq(z, sc, s):
    return sc[z.seqs + 2] * z.seqs + s


def first_kernel(z, sc, main, up, steps, down, maps, whole_o, shared_o):
    shared = z.depth + z.table_rows + z.heads_loc
    blank = jnp.zeros((z.heads_loc, z.inner_loc - z.depth), bf16)
    whole_o[0 : z.depth, :] = main[...]
    for a in range(z.owned):
        rows = slice(z.depth + a * z.rank, z.depth + (a + 1) * z.rank)
        whole_o[rows, :] = up[a, :, 1, :].astype(bf16)
        rows = slice(shared + a * z.rank, shared + (a + 1) * z.rank)
        whole_o[rows, :] = down[a].astype(bf16)
    whole_o[shared - z.heads_loc : shared, :] = jnp.concatenate([steps[...], blank], axis=1)
    shared_o[...] = whole_o[0:shared, :]
    count = z.inner_loc // (2 * z.state)
    rows = z.depth // count
    at = shared + z.table_rows
    for i in range(count):
        cols = slice(i * 2 * z.state, (i + 1) * 2 * z.state)
        whole_o[at : at + rows, cols] = maps[i * rows : (i + 1) * rows, :]


def second_kernel(z, sc, gates, out, up, down, last, whole_o):
    whole_o[0 : z.depth, :] = gates[...]
    whole_o[z.depth : 2 * z.depth, :] = out[...]
    for a in range(z.owned):
        for at, value in enumerate((up[a, :, 0, :], down[a], last[a])):
            first = 2 * z.depth + at * z.table_rows + a * z.rank
            whole_o[first : first + z.rank, :] = value.astype(bf16)


def edge_kernel(z, sc, hid, seg, spread, taps, bias, gate, skip, steps, decay, edge_o, half_o):
    for s in range(z.seqs):
        at = own_seq(z, sc, s)
        edge_o[s, :, 0 : z.width] = hid[at, z.toks - HALO :, :]
        line = jnp.broadcast_to(seg[pl.ds(at, 1), :].astype(f32) + 1.0, (LANES, z.toks))
        edge_o[s, :, z.width :] = line.T[z.toks - HALO :, :].astype(bf16)

    def lanes(row):
        return jnp.concatenate([row, jnp.zeros((1, LANES - z.heads_loc), f32)], axis=1)

    half_o[0:4, :] = taps[...]
    half_o[4:5, :] = bias[...]
    half_o[5:6, :] = gate[...]
    wide = jnp.broadcast_to(lanes(skip[...]), (8, LANES))
    half_o[6:7, :] = dot(split_heads(wide, z.heads_loc), spread[...])[0:1]
    half_o[7:9, :] = jnp.zeros((2, z.inner_loc), f32)
    half_o[7:8, 0:LANES] = lanes(steps[...])
    half_o[8:9, 0:LANES] = lanes(-jnp.exp(decay[...]))


def maps_weights(z, block):
    count = z.inner_loc // (2 * z.state)
    first = z.depth + 2 * z.table_rows + z.heads_loc
    rows = z.depth // count
    return jnp.concatenate(
        [block[first : first + rows, i * 2 * z.state : (i + 1) * 2 * z.state] for i in range(count)], axis=0
    )


def row_masks(z, wide):
    return [(pltpu.roll(wide, offset, 0)[HALO:] == wide[HALO:]).astype(f32) for offset in (1, 2, 3)]


def across(mask, width):
    return jnp.concatenate([mask] * (width // LANES), axis=1)


def conv_silu(z, m, masks, taps, bias):
    mf = m.astype(f32)
    total = bias + taps[3:4] * mf[HALO:]
    for offset in (1, 2, 3):
        moved = pltpu.roll(mf, offset, 0)[HALO:] * across(masks[offset - 1], mf.shape[1])
        total = total + taps[3 - offset : 4 - offset] * moved
    sg = sigmoid(total)
    value = total * sg
    return value, sg + value * (1.0 - sg)


def lanes_of(z, packed, index):
    moved = packed if index == 0 else pltpu.roll(packed, LANES - index * z.heads_loc, 1)
    return jnp.where(iota(packed.shape, 1) < z.heads_loc, moved, 0.0)


def forward_kernel(z, first, sc, *refs):
    refs = list(refs)

    def take(count):
        taken, refs[:count] = refs[:count], []
        return taken

    if first:
        hid, edge, seg_rows, half, spread, gain, bc_taps, bc_bias = take(8)
    else:
        seg, half, spread, normed_i, ranked_i, b_i = take(6)
    mains = take(z.shards)
    if first:
        seg, normed_i, ranked_i, b_i, c_o, slope_bc_o = take(6)
    x_o, xdt_o, slope_o, factor_o, packed_o, cumt_o = take(6)
    (states,) = take(1)
    up_s, bt_s, scale_s, masks_i = refs
    me = sc[z.seqs]
    live = iota((z.toks, LANES), 1) < z.heads_loc
    span = [slice(s * z.ext, (s + 1) * z.ext) for s in range(z.seqs)]
    if first:
        for s in range(z.seqs):
            seg[s, 0:HALO, :] = jnp.broadcast_to(edge[s, :, z.width : z.width + 1].astype(f32) - 1.0, (HALO, LANES))
            line = seg_rows[pl.ds(own_seq(z, sc, s), 1), :].astype(f32)
            seg[s, HALO:, :] = jnp.broadcast_to(line, (LANES, z.toks)).T
    for s in range(z.seqs):
        for o, mask in enumerate(row_masks(z, seg[s])):
            masks_i[s, o] = mask
    if first:
        for s in range(z.seqs):
            at = own_seq(z, sc, s)
            for low, r in ((0, edge[s, :, 0 : z.width].astype(f32)), (HALO, hid[at].astype(f32))):
                scale = lax.rsqrt(jnp.mean(r * r, axis=1, keepdims=True) + norm_eps)
                rows = slice(s * z.ext + low, s * z.ext + low + r.shape[0])
                normed_i[rows, :] = (r * scale * gain[...]).astype(bf16)
            down = table(z, mains, z.depth + z.table_rows + z.heads_loc, sc[s], me, z.width)
            ranked_i[span[s], :] = dot(normed_i[span[s], :], down, NT).astype(bf16)
        acc = None
        for r in range(z.shards):
            term = dot(normed_i[:, shard_cols(z, me, r)], maps_weights(z, mains[r]))
            acc = term if acc is None else acc + term
        for s in range(z.seqs):
            masks = [masks_i[s, o] for o in range(3)]
            v, slope = conv_silu(z, acc[span[s]].astype(bf16), masks, bc_taps[...], bc_bias[...])
            b_i[s] = v[:, : z.state].astype(bf16)
            c_o[s] = v[:, z.state :].astype(bf16)
            slope_bc_o[s] = slope.astype(bf16)
    raw = None
    at = z.depth + z.table_rows
    for r in range(z.shards):
        term = dot(normed_i[:, shard_cols(z, me, r)], mains[r][at : at + z.heads_loc, 0 : z.depth], NT)
        raw = term if raw is None else raw + term
    for s in range(z.seqs):
        bt_s[s] = b_i[s].astype(f32).T.astype(bf16)
        up_s[s] = table(z, mains, z.depth, sc[s], me, z.inner_loc)
        mine = raw[s * z.ext + HALO : (s + 1) * z.ext].astype(bf16).astype(f32)
        mine = jnp.concatenate([mine, jnp.zeros((z.toks, LANES - z.heads_loc), f32)], axis=1)
        shifted_steps = mine + half[7:8, 0:LANES]
        dt = jnp.maximum(shifted_steps, 0.0) + jnp.log1p(jnp.exp(-jnp.abs(shifted_steps)))
        dt = jnp.where(live, dt, 0.0)
        cum = running_sum(dt * half[8:9, 0:LANES]) * LOG2E
        sig = jnp.where(live, sigmoid(shifted_steps), 0.0)
        packed_o[s] = cum + pltpu.roll(dt, z.heads_loc, 1) + pltpu.roll(sig, 2 * z.heads_loc, 1)
        cumt_o[s] = cum.T[0 : z.heads_loc]
        toks = seg[s][HALO:, 0:1]
        ended = live & jnp.broadcast_to(toks == toks[z.toks - 1 :], (z.toks, LANES))
        tail = jnp.where(ended, jnp.exp2(cum[z.toks - 1 :] - cum), 0.0)
        scale_s[s, 0 : z.toks, :] = split_heads(dt, z.heads_loc)
        scale_s[s, z.toks :, :] = split_heads(tail, z.heads_loc)
        whole = live[:8] & jnp.broadcast_to(toks[z.toks - 1 :] == seg[s][HALO - 1 : HALO, 0:1], (8, LANES))
        whole = jnp.where(whole, jnp.exp2(jnp.broadcast_to(cum[z.toks - 1 :], (8, LANES))), 0.0)
        factor_o[s] = dot(split_heads(whole, z.heads_loc), spread[...])[0:1]

    def one(i, _):
        at = tile_at(i)
        acc = project(z, mains, me, normed_i, at)
        taps, bias = half[0:4, at], half[4:5, at]
        for s in range(z.seqs):
            m = (acc[span[s]] + dot(ranked_i[span[s], :], up_s[s, :, at])).astype(bf16)
            x, slope = conv_silu(z, m, [masks_i[s, o] for o in range(3)], taps, bias)
            slope_o[s, :, at] = slope.astype(bf16)
            low = x.astype(bf16)
            x_o[s, :, at] = low
            scales = dot(scale_s[s], spread[:, at])
            xdt = low.astype(f32) * scales[: z.toks]
            xdt_o[s, :, at] = xdt.astype(bf16)
            states[s, :, at] = dot(bt_s[s], (xdt * scales[z.toks :]).astype(bf16)).astype(bf16)
        return 0

    lax.fori_loop(0, z.tiles, one, 0)


def gates_kernel(z, offsets, sc, normed, ranked, *refs):
    mains, refs = refs[: z.shards], refs[z.shards :]
    others, (gates_o, toks_s, up_s) = views(refs[: z.shards], offsets), refs[z.shards :]
    me = sc[z.seqs]
    rows = [slice(s * z.toks, (s + 1) * z.toks) for s in range(z.seqs)]
    for s in range(z.seqs):
        toks_s[rows[s], :] = normed[s * z.ext + HALO : (s + 1) * z.ext, :]
        up_s[s] = table(z, others, z.depth, sc[s], me, z.inner_loc)

    def one(i):
        at = tile_at(i)
        gates = project(z, mains, me, toks_s, at)
        for s in range(z.seqs):
            ranked_s = ranked[s * z.ext + HALO : (s + 1) * z.ext, :]
            gates_o[s, :, at] = (gates[rows[s]] + dot(ranked_s, up_s[s, :, at])).astype(bf16)

    for i in range(z.tiles):
        one(i)


def ong_kernel(z, first, offsets, sc, cot, *refs):
    if first:
        mains, (small_grad_o, ong_o, down_s, cot_s) = refs[: z.shards], refs[z.shards :]
    else:
        small_grad_o, mains, (ong_o, down_s, cot_s) = refs[0], refs[1 : 1 + z.shards], refs[1 + z.shards :]
    mains = views(mains, offsets)
    me = sc[z.seqs]
    rows = [slice(s * z.toks, (s + 1) * z.toks) for s in range(z.seqs)]
    for s in range(z.seqs):
        cot_s[rows[s], :] = cot[own_seq(z, sc, s)]
        down_s[s] = table(z, mains, z.depth + z.table_rows, sc[s], me, z.inner_loc)
        if first:
            up = table(z, mains, z.depth + 2 * z.table_rows, sc[s], me, z.width)
            small_grad_o[rows[s], :] = dot(cot_s[rows[s], :], up, NT).astype(bf16)

    def one(i):
        at = tile_at(i)
        ong = project(z, mains, me, cot_s, at)
        for s in range(z.seqs):
            ong_o[s, :, at] = (ong[rows[s]] + dot(small_grad_o[rows[s], :], down_s[s, :, at])).astype(bf16)

    for i in range(z.tiles):
        one(i)


def late_kernel(z, first, offsets, sc, normed, ranked, cot, *refs):
    refs = list(refs)
    small_grad = [] if first else [refs.pop(0)]
    tops, bottoms, refs = refs[: z.shards], refs[z.shards : 2 * z.shards], refs[2 * z.shards :]
    if first:
        small_grad = [refs.pop(0)]
    gates_o, ong_o, toks_s, up_s, down_s = refs
    gates_kernel(z, offsets, sc, normed, ranked, *tops, *bottoms, gates_o, toks_s, up_s)
    if first:
        ong_kernel(z, True, offsets, sc, cot, *bottoms, *small_grad, ong_o, down_s, toks_s)
    else:
        ong_kernel(z, False, offsets, sc, cot, *small_grad, *bottoms, ong_o, down_s, toks_s)


def inside_kernel(z, sc, seg, seg_row, b, c, *refs):
    packs, cumts, xdts, outs = (refs[2 * i : 2 * i + 2] for i in range(4))
    for s in range(z.seqs):
        allowed = causal_same(seg[s][HALO:, 0:1], seg_row[pl.ds(own_seq(z, sc, s), 1), :].astype(f32), False)
        scores = jnp.where(allowed, dot(c[s], b[s], NT), 0.0)
        for k in range(z.parts):
            heads = packs[k][s]
            for g in range(z.tiles):
                tile = xdts[k][s, :, tile_at(g)]
                parts = []
                for i in range(z.heads_tile):
                    h = g * z.heads_tile + i
                    gaps = jnp.minimum(heads[:, h : h + 1] - cumts[k][s, h : h + 1, :], 0.0)
                    weighted = (jnp.exp2(gaps) * scores).astype(bf16)
                    parts.append(dot(weighted, tile[:, i * z.head_size : (i + 1) * z.head_size]))
                outs[k][s, :, tile_at(g)] = jnp.concatenate(parts, axis=1).astype(bf16)


def reach_of(z, seg, cum):
    live = iota((z.toks, LANES), 1) < z.heads_loc
    same = seg[HALO:] == seg[HALO - 1 : HALO]
    return jnp.where(live & same, jnp.exp2(cum), 0.0)


def middle_kernel(z, s, sc, *refs):
    sg_in, c, spread = refs[:3]
    packs, insides, xs, incomings, gates_i, ongs, halves = (refs[3 + 2 * i : 5 + 2 * i] for i in range(7))
    incomings = [value.at[s] for value in incomings]
    refs = refs[17:]
    ons, dys, dgs = (refs[2 * i : 2 * i + 2] for i in range(3))
    dinc_o, r_o, dc_o, y_s, gated_s, sum_s, reach_s = refs[6:]
    c_low = c[s]
    ct = c_low.astype(f32).T.astype(bf16)
    sum_s[...] = jnp.zeros_like(sum_s)
    dc_o[...] = jnp.zeros_like(dc_o)
    r_o[...] = jnp.zeros_like(r_o)
    for k in range(z.parts):
        reach_s[k] = split_heads(reach_of(z, sg_in[s], packs[k][s]), z.heads_loc)

        def first(i, k=k):
            at = tile_at(i)
            y = insides[k][s, :, at].astype(f32)
            y = y + dot(c_low, incomings[k][:, at]) * dot(reach_s[k], spread[:, at])
            y_s[k, :, at] = y
            g = gates_i[k][s, :, at].astype(f32)
            gated = (y + halves[k][6:7, at] * xs[k][s, :, at].astype(f32)) * (g * sigmoid(g))
            gated_s[k, :, at] = gated
            squares = gated * gated
            cross = gated * ongs[k][s, :, at].astype(f32) * halves[k][5:6, at]
            sum_s[0] += squares[:, :LANES] + squares[:, LANES:]
            sum_s[1] += cross[:, :LANES] + cross[:, LANES:]

        for i in range(z.tiles):
            first(i)
    inv = lax.rsqrt(jnp.sum(sum_s[0], axis=1, keepdims=True) / z.inner + norm_eps)
    pull = inv * inv * inv * jnp.sum(sum_s[1], axis=1, keepdims=True) / z.inner
    for k in range(z.parts):

        def second(i, k=k):
            at = tile_at(i)
            gated = gated_s[k, :, at]
            scaled = inv * halves[k][5:6, at]
            ons[k][:, at] = (gated * scaled).astype(bf16)
            grad = scaled * ongs[k][s, :, at].astype(f32) - gated * pull
            g = gates_i[k][s, :, at].astype(f32)
            sg = sigmoid(g)
            silu = g * sg
            y = y_s[k, :, at]
            dy = (grad * silu).astype(bf16)
            dys[k][:, at] = dy
            full = y + halves[k][6:7, at] * xs[k][s, :, at].astype(f32)
            dgs[k][:, at] = (grad * full * (sg + silu * (1.0 - sg))).astype(bf16)
            dyf = dy.astype(f32)
            carried = (dyf * dot(reach_s[k], spread[:, at])).astype(bf16)
            dinc_o[:, tile_at(k * z.tiles + i)] = dot(ct, carried).astype(bf16)
            dc_o[...] += dot(carried, incomings[k][:, at], NT)
            r_o[k] += dot((dyf * y).astype(bf16), spread[:, at], NT)

        for i in range(z.tiles):
            second(i)


def back_inside_kernel(z, s, *refs):
    sc, seg, seg_row, b, c, spread, r_fwd, dc_mid = refs[:8]
    packs, cumts, xdts, dys = (refs[8 + 2 * i : 10 + 2 * i] for i in range(4))
    refs = refs[16:]
    dxdts = refs[0:2]
    r_o, dbc_o, ds_s = refs[2:]
    allowed = causal_same(seg[s][HALO:, 0:1], seg_row[pl.ds(own_seq(z, sc, s), 1), :].astype(f32), True)
    scores = jnp.where(allowed, dot(b[s], c[s], NT), 0.0)
    ds_s[...] = jnp.zeros_like(ds_s)
    r_o[...] = r_fwd[...]
    for k in range(z.parts):

        def one(g, k=k):
            first = g * z.heads_tile
            heads = packs[k][s]
            tile, grads = xdts[k][s, :, tile_at(g)], dys[k][:, tile_at(g)]
            parts = []
            total = None
            for i in range(z.heads_tile):
                cols = slice(i * z.head_size, (i + 1) * z.head_size)
                gaps = jnp.minimum(cumts[k][s, first + i : first + i + 1, :] - heads[:, first + i : first + i + 1], 0.0)
                decay = jnp.exp2(gaps)
                weighted = (decay * scores).astype(bf16)
                parts.append(dot(weighted, grads[:, cols]))
                term = decay * dot(tile[:, cols], grads[:, cols], NT)
                total = term if total is None else total + term
            ds_s[...] += total
            dxdt = jnp.concatenate(parts, axis=1)
            dxdts[k][:, tile_at(g)] = dxdt.astype(bf16)
            r_o[k] -= dot((tile.astype(f32) * dxdt).astype(bf16), spread[:, tile_at(g)], NT)

        for i in range(z.tiles):
            one(i)
    ds = jnp.where(allowed, ds_s[...], 0.0).astype(bf16)
    dbc_o[:, 0 : z.state] = dot(ds, c[s])
    dbc_o[:, z.state :] = dot(ds, b[s], TN) + dc_mid[...]


def finish_kernel(z, s, *refs):
    sc, seg, b, spread, bc_taps, slope_bc, dbc, r_in = refs[:8]
    refs = refs[8:]
    names = 8
    (packs, halves, xs, xdts, slopes, dys, dxdts, incomings) = (refs[2 * i : 2 * i + 2] for i in range(names))
    incomings = [value.at[s] for value in incomings]
    later, refs = refs[2 * names], refs[2 * names + 1 :]
    dms = refs[0:2]
    draw_o, dm_bc_o, masks_s, scale_s, e_s, ddt_s, db_s, dec_s = refs[2:]
    toks = seg[s][HALO:]
    live = iota((z.toks, LANES), 1) < z.heads_loc
    ended = live & (toks == toks[z.toks - 1 :])
    for o, mask in enumerate(row_masks(z, seg[s])):
        masks_s[o] = mask
    db_s[...] = dbc[:, 0 : z.state]

    def unconv(dpre, taps):
        blank = jnp.zeros((HALO, dpre.shape[1]), f32)
        total = jnp.concatenate([blank, taps[3:4] * dpre], axis=0)
        for offset in (1, 2, 3):
            term = taps[3 - offset : 4 - offset] * (dpre * across(masks_s[offset - 1], dpre.shape[1]))
            total = total + pltpu.roll(jnp.concatenate([blank, term], axis=0), z.ext - offset, 0)
        return total.astype(bf16)

    for k in range(z.parts):
        packed = packs[k][s]
        cum = lanes_of(z, packed, 0)
        tail = jnp.where(ended, jnp.exp2(cum[z.toks - 1 :] - cum), 0.0)
        scale_s[0 : z.toks, :] = split_heads(lanes_of(z, packed, 1), z.heads_loc)
        scale_s[z.toks :, :] = split_heads(tail, z.heads_loc)
        e_s[...] = jnp.zeros_like(e_s)
        ddt_s[...] = jnp.zeros_like(ddt_s)
        dec_s[...] = jnp.zeros_like(dec_s)

        def one(i, k=k):
            at = tile_at(i)
            low = xdts[k][s, :, at]
            d = later[:, tile_at(k * z.tiles + i)]
            scales = dot(scale_s[...], spread[:, at])
            tails = scales[z.toks :]
            lowf = low.astype(f32)
            last = dot(b[s], d) * tails
            db_s[...] += dot((lowf * tails).astype(bf16), d, NT)
            e_s[...] += dot((lowf * last).astype(bf16), spread[:, at], NT)
            dxdt = dxdts[k][:, at].astype(f32) + last
            ddt_s[...] += dot((dxdt * xs[k][s, :, at].astype(f32)).astype(bf16), spread[:, at], NT)
            dx = dxdt * scales[: z.toks] + halves[k][6:7, at] * dys[k][:, at].astype(f32)
            dms[k][:, at] = unconv(dx * slopes[k][s, :, at].astype(f32), halves[k][0:4, at])
            both = d.astype(f32) * incomings[k][:, at].astype(f32)
            summed = jnp.broadcast_to(jnp.sum(both, axis=0, keepdims=True), (8, TILE))
            dec_s[...] += dot(summed.astype(bf16), spread[:, at], NT)

        for i in range(z.tiles):
            one(i)
        e = e_s[...]
        reach_last = reach_of(z, seg[s], cum)[z.toks - 1 :]
        last = jnp.sum(e, axis=0, keepdims=True) + reach_last * dec_s[0:1]
        grad_cum = r_in[k] - e
        grad_cum = grad_cum + jnp.where(iota((z.toks, LANES), 0) == z.toks - 1, last, 0.0)
        grad_decay = running_sum(grad_cum, True)
        steps = (ddt_s[...] + halves[k][8:9, 0:LANES] * grad_decay) * lanes_of(z, packed, 2)
        draw_o[k] = jnp.where(live, steps, 0.0).astype(bf16)
    grad_bc = jnp.concatenate([db_s[...], dbc[:, z.state :]], axis=1)
    dm_bc_o[...] = unconv(grad_bc * slope_bc[s].astype(f32), bc_taps[...])


def both_parts(z, refs):
    return [refs[k * z.shards : (k + 1) * z.shards] for k in range(z.parts)], refs[z.parts * z.shards :]


def output_kernel(z, offsets, sc, hid, cot, small_grad, *refs):
    ons, refs = refs[: 2 * z.seqs], refs[2 * z.seqs :]
    outs, refs = both_parts(z, refs)
    outs = [views(outs[k], offsets[k]) for k in range(z.parts)]
    out_o, (gdown_o, gup_o, up_s, on_s) = refs[: z.seqs], refs[z.seqs :]
    me = sc[z.seqs]
    smalls = []
    for s in range(z.seqs):
        rows = slice(s * z.toks, (s + 1) * z.toks)
        small = None
        for k in range(z.parts):
            on = ons[s * z.parts + k][...]
            on_s[k, rows, :] = on
            gdown_o[s, :, k * z.inner_loc : (k + 1) * z.inner_loc] = dot(small_grad[rows, :], on, TN)
            term = dot(on, table(z, outs[k], z.depth + z.table_rows, sc[s], me, z.inner_loc), NT)
            small = term if small is None else small + term
        smalls.append(small.astype(bf16))
        gup_o[s] = dot(smalls[s], cot[own_seq(z, sc, s)], TN)
        up_s[s] = table(z, outs[0], z.depth + 2 * z.table_rows, sc[s], me, z.width)
    for r in range(z.shards):
        cols = shard_cols(z, me, r)
        acc = None
        for k in range(z.parts):
            term = dot(on_s[k], outs[k][r][0 : z.depth, :], NT)
            acc = term if acc is None else acc + term
        for s in range(z.seqs):
            whole = hid[own_seq(z, sc, s), :, cols].astype(f32) + dot(smalls[s], up_s[s, :, cols])
            out_o[s][:, cols] = (whole + acc[s * z.toks : (s + 1) * z.toks]).astype(bf16)


def gates_back_kernel(z, offsets, sc, ranked, *refs):
    dgs, refs = refs[: 2 * z.seqs], refs[2 * z.seqs :]
    mains, refs = both_parts(z, refs)
    others, (ngrad_o, rank_o, gup_o, dg_s) = both_parts(z, refs)
    others = [views(others[k], offsets[k]) for k in range(z.parts)]
    me = sc[z.seqs]
    for s in range(z.seqs):
        ranked_s = ranked[s * z.ext + HALO : (s + 1) * z.ext, :]
        rank = None
        for k in range(z.parts):
            dg = dgs[s * z.parts + k][...]
            dg_s[k, s * z.toks : (s + 1) * z.toks, :] = dg
            gup_o[s, :, k * z.inner_loc : (k + 1) * z.inner_loc] = dot(ranked_s, dg, TN)
            term = dot(dg, table(z, others[k], z.depth, sc[s], me, z.inner_loc), NT)
            rank = term if rank is None else rank + term
        rank_o[s] = rank
    for r in range(z.shards):
        acc = None
        for k in range(z.parts):
            term = dot(dg_s[k], mains[k][r][0 : z.depth, :], NT)
            acc = term if acc is None else acc + term
        for s in range(z.seqs):
            ngrad_o[s, :, shard_cols(z, me, r)] = acc[s * z.toks : (s + 1) * z.toks]


def rank_kernel(z, s, chunks, sc, normed, ranked, rank_gates, g_gates, g_out_down, g_out_up, dm_own, dm_other, *refs):
    mains, refs = both_parts(z, refs)
    if s:
        before, refs = refs[:chunks], refs[chunks:]
    rank_o, grads_o, all_s = refs[0], refs[1 : 1 + chunks], refs[1 + chunks]
    me = sc[z.seqs]
    dms = (dm_own, dm_other)
    span = slice(s * z.ext, (s + 1) * z.ext)
    chunk = z.inner_loc // chunks

    def keep(block, value):
        all_s[block * z.rank : (block + 1) * z.rank, :] = value

    for k in range(z.parts):
        cols = slice(k * z.inner_loc, (k + 1) * z.inner_loc)
        keep(1 + k, g_gates[s, :, cols])
        keep(1 + z.parts + k, dot(ranked[span, :], dms[k][...], TN))
        keep(1 + 2 * z.parts + k, g_out_down[s, :, cols])
    keep(1 + 3 * z.parts, g_out_up[s])
    rank = jnp.concatenate([jnp.zeros((HALO, z.rank), f32), rank_gates[s]], axis=0)
    for k in range(z.parts):
        rank = rank + dot(dms[k][...], table(z, mains[k], z.depth, sc[s], me, z.inner_loc), NT)
    rank = rank.astype(bf16)
    rank_o[...] = rank
    keep(0, dot(rank, normed[span, :], TN))
    turned = pltpu.roll(all_s[...], lax.rem(chunks - sc[z.seqs + 1], chunks) * chunk, 1).astype(bf16)
    for i in range(chunks):
        mine = turned[:, i * chunk : (i + 1) * chunk]
        if s:
            for earlier in range(s):
                grads_o[i][earlier] = before[i][...]
            grads_o[i][s] = mine
        else:
            grads_o[i][...] = mine


def kept_kernel(z, sc, *refs):
    pieces, kept_o = refs[: -z.parts], refs[-z.parts :]
    total = pieces[0][...].astype(f32)
    for piece in pieces[1:]:
        total = total + piece[...].astype(f32)
    total = total.astype(bf16)
    for part in range(z.parts):
        picks = [0] + [1 + z.parts * i + part for i in range(3)] + [1 + 3 * z.parts]
        for to, pick in enumerate(picks):
            rows = slice(pick * z.rank, (pick + 1) * z.rank)
            kept_o[part][:, to * z.rank : (to + 1) * z.rank, :] = total[:, rows, :]


def chosen_kernel(z, sc, mine, other, *outs):
    base = z.seqs + 3
    me, tp = sc[z.seqs], sc[z.seqs + 2]
    for r in range(z.shards):
        for a in range(z.owned):
            want = lax.bitwise_xor(me, r) * z.owned + a
            total = jnp.zeros(mine.shape[1:], f32)
            for values, part in ((mine, tp), (other, 1 - tp)):
                for s in range(z.seqs):
                    here = sc[base + part * z.seqs + s] == want
                    total = total + jnp.where(here, values[s].astype(f32), 0.0)
            outs[r][a] = total.astype(bf16)


def owned_kernel(z, sc, *refs):
    total = refs[0][...].astype(f32)
    for piece in refs[1:-1]:
        total = total + piece[...].astype(f32)
    refs[-1][...] = total.astype(bf16)


def adam_kernel(z, chunks, sc, *refs):
    pieces, refs = refs[:chunks], refs[chunks:]
    params, outs = refs[:12], refs[12:]
    chunk = z.inner_loc // chunks
    rates = (rate_down, rate_up, rate_down, rate_up)
    for a in range(z.owned):
        joined = jnp.concatenate([pieces[0][a]] + [pieces[chunks - i][a] for i in range(1, chunks)], axis=1)
        grads = pltpu.roll(joined.astype(f32), sc[z.seqs + 1] * chunk, 1)
        for t in range(4):
            for i in range(2 if t == 1 else 1):
                block = (0, 1 + i, 3, 4)[t]
                grad = grads[block * z.rank : (block + 1) * z.rank]
                at = (a, slice(None), i, slice(None)) if t == 1 else (a,)
                new = adam_update(*(params[4 * j + t][at] for j in range(3)), grad, rates[t])
                for j in range(3):
                    outs[4 * j + t][at] = new[j]


def input_kernel(z, s, sc, rank_i, dm_own, dm_other, dm_bc, draw, ngrad_gates, *refs):
    mains, (ngrad_o, halo_o, down_s) = both_parts(z, refs)
    me = sc[z.seqs]
    dms = (dm_own, dm_other)
    down_s[...] = table(z, mains[0], z.depth + z.table_rows + z.heads_loc, sc[s], me, z.width)
    at = z.depth + z.table_rows
    for r in range(z.shards):
        cols = shard_cols(z, me, r)
        acc = dot(rank_i[...], down_s[:, cols]) + dot(dm_bc[...], maps_weights(z, mains[0][r]), NT)
        steps = None
        for k in range(z.parts):
            acc = acc + dot(dms[k][...], mains[k][r][0 : z.depth, :], NT)
            term = dot(draw[k][:, 0 : z.heads_loc], mains[k][r][at : at + z.heads_loc, 0 : z.depth])
            steps = term if steps is None else steps + term
        halo_o[:, cols] = acc[0:HALO].astype(bf16)
        ngrad_o[:, cols] = acc[HALO:] + steps + ngrad_gates[s, :, cols]


def close_kernel(z, s, sc, ngrad, back, hid, cot, gain, out_o):
    rows = hid[own_seq(z, sc, s)].astype(f32)
    grad = ngrad[...]
    ends = back[...].astype(f32)
    grad = grad + jnp.concatenate([jnp.zeros((z.toks - HALO, z.width), f32), ends], axis=0)
    scale = lax.rsqrt(jnp.mean(rows * rows, axis=1, keepdims=True) + norm_eps)
    scaled = grad * gain[...]
    inner = jnp.mean(scaled * rows, axis=1, keepdims=True)
    moved = scale * scaled - rows * (scale * scale * scale * inner)
    out_o[...] = (cot[own_seq(z, sc, s)].astype(f32) + moved).astype(bf16)


def call(kernel, outs, args, scratch=(), name=None):
    args = list(args)
    return pl.pallas_call(
        kernel,
        out_shape=[jax.ShapeDtypeStruct(o.shape, o.dtype) for o in outs],
        in_specs=[pl.BlockSpec(memory_space=pltpu.SMEM)] + [pl.BlockSpec(memory_space=pltpu.VMEM)] * (len(args) - 1),
        out_specs=[pl.BlockSpec(memory_space=pltpu.VMEM)] * len(outs),
        scratch_shapes=list(scratch),
        compiler_params=pltpu.CompilerParams(vmem_limit_bytes=VMEM_BYTES),
        cost_estimate=pl.CostEstimate(flops=1024, bytes_accessed=1024, transcendentals=0),
        name=name,
    )(*args)


def spec(shape, dtype):
    return jax.ShapeDtypeStruct(shape, dtype)


def swap_parts(value):
    count = lax.axis_size("tp")
    return lax.ppermute(value, "tp", [(i, (i + 1) % count) for i in range(count)])


def swap_shards(value, bit):
    return lax.ppermute(value, "shard", [(i, i ^ bit) for i in range(lax.axis_size("shard"))])


def place_kernel(z, sc, *refs):
    mine, other, (out, sems) = refs[: z.seqs], refs[z.seqs : 2 * z.seqs], refs[2 * z.seqs :]
    tp = sc[z.seqs + 2]
    copies = []
    for part, values in ((tp, mine), (1 - tp, other)):
        for s in range(z.seqs):
            to = out.at[part * z.seqs + s]
            copies.append(pltpu.make_async_copy(values[s], to, sems.at[len(copies)]))
            copies[-1].start()
    for copy in copies:
        copy.wait()


def in_place(z, scalars, mine, other):
    shape = (z.seqs_loc,) + mine[0].shape
    return pl.pallas_call(
        functools.partial(place_kernel, z),
        out_shape=jax.ShapeDtypeStruct(shape, mine[0].dtype),
        in_specs=[pl.BlockSpec(memory_space=pltpu.SMEM)] + [pl.BlockSpec(memory_space=pltpu.VMEM)] * (2 * z.seqs),
        out_specs=pl.BlockSpec(memory_space=pltpu.HBM),
        scratch_shapes=[pltpu.SemaphoreType.DMA((2 * z.seqs,))],
        compiler_params=pltpu.CompilerParams(vmem_limit_bytes=VMEM_BYTES),
        cost_estimate=pl.CostEstimate(flops=1024, bytes_accessed=1024, transcendentals=0),
        name="place",
    )(scalars, *mine, *other)


class Waves:
    def __init__(self, value, factor, places, down):
        self.count = lax.axis_size("ctx")
        self.first, self.places, self.down = (value, factor), places if down else places[::-1], down
        self.came, self.sent = [], value
        self.send(value)

    def send(self, value):
        wave = len(self.came)
        pairs = [(at, at + 1) for at in (wave, wave - 1) if 0 <= at < self.count - 1]
        if not self.down:
            pairs = [(self.count - 1 - a, self.count - 1 - b) for a, b in pairs]
        self.sent = value
        self.came.append(lax.ppermute(value, "ctx", pairs))

    def join(self, value, factor):
        self.second = (value, factor)

    def step(self, *earlier):
        wave = len(self.came)
        if wave < self.count:
            came = after(self.came[-1], *earlier).astype(f32)
            mixed = [factor * came + value.astype(f32) for value, factor in (self.first, self.second)]
            here = self.places[wave : wave + 1].reshape((1,) * came.ndim)
            self.send((here * mixed[0] + (1.0 - here) * mixed[1]).astype(bf16))
        return self.sent

    def total(self, which, *earlier):
        while len(self.came) < self.count - 1 + which:
            self.step(*earlier)
        total = None
        for wave in range(which, self.count - 1 + which):
            at = wave + 1 - which
            came = self.came[wave]
            if wave == self.count - 2 + which:
                came = after(came, *earlier)
            here = self.places[at : at + 1].reshape((1,) * came.ndim)
            term = here * came.astype(f32)
            total = term if total is None else total + term
        return total.astype(bf16)


def after(value, *earlier):
    return lax.optimization_barrier((value, earlier))[0] if earlier else value


def adam_update(weight, first, second, gradient, rate):
    first_new = beta_one * first + (1.0 - beta_one) * gradient
    second_new = beta_two * second + (1.0 - beta_two) * gradient * gradient
    first_hat = first_new / (1.0 - beta_one**STEP)
    second_hat = second_new / (1.0 - beta_two**STEP)
    weight_new = weight - rate * (
        first_hat / (jnp.sqrt(second_hat) + adam_eps) + weight_decay * weight
    )
    return (weight_new, first_new, second_new)


def shifted(value, axis, by):
    count = lax.axis_size(axis)
    return lax.ppermute(value, axis, [(i, (i + by) % count) for i in range(count)])


def local(
    hidden,
    cotangent,
    segment_ids,
    adapter_ids,
    norm_gain,
    proj_zx,
    proj_bc,
    proj_dt,
    proj_out,
    conv_x,
    conv_x_bias,
    conv_bc,
    conv_bc_bias,
    dt_bias,
    decay_log,
    skip_gain,
    gate_gain,
    in_down,
    in_up,
    out_down,
    out_up,
    in_down_m,
    in_up_m,
    out_down_m,
    out_up_m,
    in_down_v,
    in_up_v,
    out_down_v,
    out_up_v,
):
    parts = lax.axis_size("tp")
    z = Sizes(hidden, proj_zx, conv_bc, dt_bias, in_down, lax.axis_size("shard"), parts)
    tp = lax.axis_index("tp")
    sq, tk, ex, inner = z.seqs, z.toks, z.ext, z.inner_loc

    def turn(table):
        return jnp.swapaxes(table, 1, 2)

    def flat_low(table):
        return table.reshape(z.table_rows, -1).astype(bf16)

    ids = lax.dynamic_slice_in_dim(adapter_ids, tp * z.seqs, z.seqs, axis=0)
    places = [lax.axis_index(name)[None].astype(jnp.int32) for name in ("shard", "ctx", "tp")]
    scalars = jnp.concatenate([ids] + places + [adapter_ids])
    here = (jnp.arange(lax.axis_size("ctx")) == lax.axis_index("ctx")).astype(f32)
    shared = z.depth + z.table_rows + z.heads_loc
    first, first_shared = call(
        functools.partial(first_kernel, z),
        [
            spec((shared + z.table_rows + z.depth * 2 * z.state // inner, inner), bf16),
            spec((shared, inner), bf16),
        ],
        [scalars, proj_zx[:, 1, :], in_up, proj_dt.T, turn(in_down), proj_bc],
        name="first",
    )
    ins = Gather(first)
    (second,) = call(
        functools.partial(second_kernel, z),
        [spec((2 * z.depth + 3 * z.table_rows, inner), bf16)],
        [scalars, after(proj_zx, first)[:, 0, :], proj_out, in_up, turn(out_down), out_up],
        name="second",
    )
    late = Gather(second)
    lane = np.arange(LANES)[:, None]
    place = np.arange(inner)[None, :] // z.head_size
    spread = jnp.asarray((lane % z.heads_loc == place) & (lane < 3 * z.heads_loc), bf16)
    own_rows = [conv_x_bias[None], gate_gain[None], skip_gain[None], dt_bias[None], decay_log[None]]
    edge, half = call(
        functools.partial(edge_kernel, z),
        [spec((sq, HALO, z.width + LANES), bf16), spec((9, inner), f32)],
        [after(scalars, first), hidden, segment_ids, spread, conv_x] + own_rows,
        name="edge",
    )
    count = lax.axis_size("ctx")
    half_far = z.shards // 2
    ins.far_own()
    ins.part(first_shared)
    edge = lax.ppermute(edge, "ctx", [(i, i + 1) for i in range(count - 1)])
    halves = (half, swap_parts(half))
    ins.near(ins.own, False, edge)
    ins.near(ins.own, True, halves[1], edge, ins.other[0])
    ins.far_by_part(shared, ins.other[0], edge)
    late.near(late.own, False, halves[1])
    late.far_own(ins.own[half_far])
    ins.near(ins.other, False)
    scalars, here = after((scalars, here), halves[1], late.own[1])
    gain = norm_gain[None]

    half_outs = [
        spec((sq, tk, inner), bf16),
        spec((sq, tk, inner), bf16),
        spec((sq, tk, inner), bf16),
        spec((sq, 1, inner), f32),
        spec((sq, tk, LANES), f32),
        spec((sq, z.heads_loc, tk), f32),
    ]
    half_scratch = [
        pltpu.VMEM((sq, z.rank, inner), bf16),
        pltpu.VMEM((sq, z.state, tk), bf16),
        pltpu.VMEM((sq, 2 * tk, LANES), bf16),
        pltpu.VMEM((sq, 3, tk, LANES), f32),
    ]
    in_own = ins.blocks(ins.own)
    seg, normed, ranked, b, c, slope_bc, *fwd_own = call(
        functools.partial(forward_kernel, z, True),
        [
            spec((sq, ex, LANES), f32),
            spec((sq * ex, z.width), bf16),
            spec((sq * ex, z.rank), bf16),
            spec((sq, tk, z.state), bf16),
            spec((sq, tk, z.state), bf16),
            spec((sq, tk, 2 * z.state), bf16),
        ]
        + half_outs
        + [spec((sq, z.state, inner), bf16)],
        [scalars, hidden, edge, segment_ids, half, spread, gain, conv_bc, conv_bc_bias[None]] + in_own,
        scratch=half_scratch,
        name="forward_own",
    )
    waves = Waves(fwd_own[6], fwd_own[3], here, True)
    ran = fwd_own[0]
    ins.near(ins.other, True, ran)
    late.part(second, ran)

    def late_part(k, extra, *earlier):
        tops, bottoms, offsets = late.halves(k, z.depth)
        return call(
            functools.partial(late_kernel, z, k == 0, offsets),
            ([spec((sq * tk, z.rank), bf16)] if k == 0 else []) + [spec((sq, tk, inner), bf16)] * 2,
            [after(scalars, *earlier), normed, ranked, cotangent] + extra + tops + bottoms,
            scratch=[
                pltpu.VMEM((sq * tk, z.width), bf16),
                pltpu.VMEM((sq, z.rank, inner), bf16),
                pltpu.VMEM((sq, z.rank, inner), bf16),
            ],
            name="late",
        )

    fwd_other = call(
        functools.partial(forward_kernel, z, False),
        half_outs + [spec((sq, z.state, inner), bf16)],
        [scalars, seg, halves[1], spread, normed, ranked, b] + ins.blocks(ins.other),
        scratch=half_scratch,
        name="forward_other",
    )
    waves.join(fwd_other[6], fwd_other[3])
    xs, xdts, slopes, factors, packs, cumts = list(zip(fwd_own, fwd_other))[:6]
    waved = waves.step(fwd_other[0])
    insides = call(
        functools.partial(inside_kernel, z),
        [spec((sq, tk, inner), bf16)] * parts,
        [after(scalars, waved), seg, segment_ids, b, c, *packs, *cumts, *xdts],
        name="inside",
    )
    late.near(late.own, True, insides[0])
    late.far_top(z.depth, insides[0])
    waved = waves.step(insides[0])
    late.far_bottom(z.depth, waved)
    late.near(late.other, False, waved)
    small_grad, gates_own, ong_own = late_part(0, [], waved)
    waved = waves.step(ong_own)
    late.near(late.top, True, waved)
    late.near(late.bottom, True, waved)
    incomings = [waves.total(k, ong_own) for k in range(parts)]
    gates_other, ong_other = late_part(1, [small_grad], *incomings)
    gates, ongs = (gates_own, gates_other), (ong_own, ong_other)
    tops, bottoms, offsets = zip(*(late.halves(k, z.depth) for k in range(parts)))
    tops, bottoms = sum(tops, []), sum(bottoms, [])
    in_blocks = in_own + ins.blocks(ins.other)

    wide = [spec((tk, inner), bf16)] * 2
    heads = spec((parts, tk, LANES), f32)
    middles = []
    for s in range(sq):
        got = call(
            functools.partial(middle_kernel, z, s),
            wide + wide + wide + [spec((z.state, z.inner), bf16), heads, spec((tk, z.state), f32)],
            [scalars, seg, c, spread, *packs, *insides, *xs, *incomings, *gates, *ongs, *halves],
            scratch=[
                pltpu.VMEM((parts, tk, inner), f32),
                pltpu.VMEM((parts, tk, inner), f32),
                pltpu.VMEM((2, tk, LANES), f32),
                pltpu.VMEM((parts, tk, LANES), bf16),
            ],
            name="middle",
        )
        factor = jnp.concatenate([factors[k][s] for k in range(parts)], axis=1)
        if s == 0:
            back_waves = Waves(got[6], factor, here, False)
        else:
            back_waves.join(got[6], factor)
        middles.append((got[0:2], got[2:4], got[4:6], got[7], got[8]))

    def back_inside(s, *earlier):
        ons, dys, dgs, r_fwd, dc_mid = middles[s]
        return call(
            functools.partial(back_inside_kernel, z, s),
            wide + [heads, spec((tk, 2 * z.state), f32)],
            [after(scalars, *earlier), seg, segment_ids, b, c, spread, r_fwd, dc_mid, *packs, *cumts, *xdts, *dys],
            scratch=[pltpu.VMEM((tk, tk), f32)],
            name="back_inside",
        )

    def output_part(*earlier):
        return call(
            functools.partial(output_kernel, z, offsets),
            [spec((tk, z.width), bf16)] * sq
            + [spec((sq, z.rank, z.inner), f32), spec((sq, z.rank, z.width), f32)],
            [after(scalars, *earlier), hidden, cotangent, small_grad] + [on for m in middles for on in m[0]] + bottoms,
            scratch=[pltpu.VMEM((sq, z.rank, z.width), bf16), pltpu.VMEM((parts, sq * tk, inner), bf16)],
            name="output",
        )

    def gates_back(*earlier):
        return call(
            functools.partial(gates_back_kernel, z, offsets),
            [spec((sq, tk, z.width), f32), spec((sq, tk, z.rank), f32), spec((sq, z.rank, z.inner), f32)],
            [after(scalars, *earlier), ranked] + [dg for m in middles for dg in m[2]] + tops + bottoms,
            scratch=[pltpu.VMEM((parts, sq * tk, inner), bf16)],
            name="gates_back",
        )

    def finish(s, got, later, *earlier):
        return call(
            functools.partial(finish_kernel, z, s),
            [spec((ex, inner), bf16)] * 2 + [spec((parts, tk, LANES), bf16), spec((ex, 2 * z.state), bf16)],
            [after(scalars, *earlier), seg, b, spread, conv_bc, slope_bc, got[3], got[2], *packs, *halves, *xs,
             *xdts, *slopes, *middles[s][1], *got[0:2], *incomings, later],
            scratch=[
                pltpu.VMEM((3, tk, LANES), f32),
                pltpu.VMEM((2 * tk, LANES), bf16),
                pltpu.VMEM((tk, LANES), f32),
                pltpu.VMEM((tk, LANES), f32),
                pltpu.VMEM((tk, z.state), f32),
                pltpu.VMEM((8, LANES), f32),
            ],
            name="finish",
        )

    grad_rows = (2 + 3 * parts) * z.rank
    chunk = inner // count

    def rank_part(s, dms, before, *earlier):
        shape = (s + 1, grad_rows, chunk) if s else (grad_rows, chunk)
        rank, *pieces = call(
            functools.partial(rank_kernel, z, s, count),
            [spec((ex, z.rank), bf16)] + [spec(shape, bf16)] * count,
            [after(scalars, *earlier), normed, ranked, *gate_grads[1:], *out_grads, *dms] + in_blocks + list(before),
            scratch=[pltpu.VMEM((grad_rows, inner), f32)],
            name="rank",
        )
        return rank, pieces

    def input_part(s, rank, dms, dm_bc, draw, *earlier):
        return call(
            functools.partial(input_kernel, z, s),
            [spec((tk, z.width), f32), spec((HALO, z.width), bf16)],
            [after(scalars, *earlier), rank, *dms, dm_bc, draw, gate_grads[0]] + in_blocks,
            scratch=[pltpu.VMEM((z.rank, z.width), bf16)],
            name="input",
        )

    def sent_back(halo, *earlier):
        return lax.ppermute(after(halo, *earlier), "ctx", [(i + 1, i) for i in range(count - 1)])

    def close(s, ngrad, back, *earlier):
        (own,) = call(
            functools.partial(close_kernel, z, s),
            [spec((tk, z.width), bf16)],
            [after(scalars, *earlier), ngrad, back, hidden, cotangent, gain],
            name="close",
        )
        return own

    assert sq == 2
    got = output_part()
    output_own, out_grads = got[:sq], got[sq:]
    output_other = [swap_parts(value) for value in output_own]
    backs = [back_inside(0, back_waves.step(output_own[0]))]
    backs.append(back_inside(1, back_waves.step(backs[0][0])))
    gate_grads = gates_back(backs[1][0])
    back_waves.step(gate_grads[0])
    dm_own, dm_other, draw, dm_bc = finish(0, backs[0], back_waves.total(0, gate_grads[0]))
    rank, pieces = rank_part(0, (dm_own, dm_other), [])
    ngrad, halo = input_part(0, rank, (dm_own, dm_other), dm_bc, draw)
    dm_own, dm_other, draw, dm_bc = finish(1, backs[1], back_waves.total(1, ngrad), *output_other)
    closed = [close(0, ngrad, sent_back(halo), dm_own)]
    closed_other = [swap_parts(closed[0])]
    rank, pieces = rank_part(1, (dm_own, dm_other), pieces, closed[0])
    came = [shifted(pieces[by], "ctx", by) for by in range(1, count)]
    ngrad, halo = input_part(1, rank, (dm_own, dm_other), dm_bc, draw)
    back = sent_back(halo)
    kept_rows = 5 * z.rank
    kept = spec((sq, kept_rows, chunk), bf16)
    mine, theirs = call(
        functools.partial(kept_kernel, z),
        [kept] * parts,
        [after(scalars, ngrad, closed_other[0]), pieces[0]] + came,
        name="kept",
    )
    theirs = swap_parts(theirs)
    closed.append(close(1, ngrad, back, mine))
    closed_other.append(swap_parts(after(closed[1], theirs)))
    share = spec((z.owned, kept_rows, chunk), bf16)
    shares = call(
        functools.partial(chosen_kernel, z),
        [share] * z.shards,
        [after(scalars, closed[1]), mine, theirs],
        name="chosen",
    )
    came = [swap_shards(shares[r], r) for r in range(1, z.shards)]
    (total,) = call(functools.partial(owned_kernel, z), [share], [scalars, shares[0]] + came, name="owned")
    output = in_place(z, after(scalars, total), output_own, output_other)
    came = [shifted(total, "ctx", by) for by in range(1, count)]

    params = []
    for tables in ((in_down, in_up, out_down, out_up), (in_down_m, in_up_m, out_down_m, out_up_m),
                   (in_down_v, in_up_v, out_down_v, out_up_v)):
        params += [turn(tables[0]), tables[1], turn(tables[2]), tables[3]]
    new = call(
        functools.partial(adam_kernel, z, count),
        [spec(p.shape, f32) for p in params],
        [after(scalars, output), total] + came + params,
        name="adam",
    )
    input_grad = in_place(z, after(scalars, new[0]), closed, closed_other)
    return (output, input_grad) + tuple(turn(p) if t % 2 == 0 else p for t, p in enumerate(new))


def solution(mesh):
    rows = P("shard", "ctx", None)
    table_specs = (
        P("shard", None, None),
        P("shard", None, None, "tp"),
        P("shard", "tp", None),
        P("shard", None, None),
    )
    return jax.shard_map(
        local,
        mesh=mesh,
        in_specs=(
            rows,
            rows,
            P("shard", "ctx"),
            P("shard"),
            P(),
            P("shard", None, "tp"),
            P("shard", None),
            P("shard", "tp"),
            P("shard", "tp"),
            P(None, "tp"),
            P("tp"),
            P(),
            P(),
            P("tp"),
            P("tp"),
            P("tp"),
            P("tp"),
        )
        + table_specs * 3,
        out_specs=(rows, rows) + table_specs * 3,
        check_vma=False,
    )
```
